512 devices in a mesh: section: 8 (over x, core), expert: 64 (over y, z).
Axes of the slice: x: 4, y: 8, z: 8, core: 2. Of those that a mesh axis runs over, the one named last changes fastest.
Arguments:
- grad_codes: bfloat16 [8, 8192, 4096], P('section', 'expert'), may hold values from -127 to 127, as said below
- grad_scales: bfloat16 [8, 8192], P('section', 'expert'), may hold values from 0.0009994507 to 0.0099487305
- routes: int32 [8, 8192, 2], P('section', 'expert'), may hold values from 0 to 15, as said below
- router_logits: float32 [8, 8192, 16], P('section', 'expert'), may hold values from -12 to 310
- expert_outputs: bfloat16 [8, 64, 1536, 1024], P('section', 'expert'), may hold values from -1.1953125 to 1.1953125
Outputs:
- logit_grad: float32 [8, 8192, 16], P('section', 'expert')
The draws below stay inside these ranges and needn't reach their ends.
Inputs may be any that keep to these rules, and one draw needn't show every extreme that they name: `grad_codes`: integer values. `routes`: each token names two different experts; among the rows of one device no expert is named more than 24 times, and in each section some expert is named exactly 24 times on every device.
All inputs are finite; a program needn't handle non-finite values.
Results may differ from the reference program's by a relative error of at most 0.009.
Values may be sent and summed in bfloat16 or wider, within the bound.
No kernel may reach another device: no remote copies, remote signals or barrier semaphores. Data moves between devices by JAX's collectives and lax.ppermute only.
A program may use at most 64 MiB of HBM per device.

```python
import math
import jax
import jax.numpy as jnp
from jax import lax

DW = 4096
EXPERTS = 16
TOK_DEV = 128
SECTIONS = 8
OWNERS = 64
TOKENS = 8192
DWQ = 1024
CAP = 24


def draw_grad_codes(key, part):
    key = jax.random.fold_in(key, 3)
    values = jax.random.randint(key, (SECTIONS, TOKENS, DW), -127, 128)
    return values.astype(jnp.float32).astype(jnp.bfloat16)


def route_block(key, hottest):
    key_rank, key_rows = jax.random.split(key)
    expert_ids = jnp.arange(EXPERTS, dtype=jnp.int32)
    ranking = jax.random.permutation(key_rank, EXPERTS).astype(jnp.int32)
    hot_rank = jnp.sum(jnp.where(expert_ids == hottest, ranking, 0))
    ranking = jnp.where(expert_ids == hottest, EXPERTS - 1, jnp.where(ranking == EXPERTS - 1, hot_rank, ranking))
    spare = 2 * TOK_DEV - CAP
    base_load = spare // (EXPERTS - 1)
    leftover = spare - base_load * (EXPERTS - 1)
    half_load = base_load // 2
    lift = jnp.where(ranking < leftover, 1, 0)
    swing = jnp.where(ranking < EXPERTS - 2, jnp.where(ranking % 2 == 0, half_load, -half_load), 0)
    loads = jnp.where(ranking == EXPERTS - 1, CAP, base_load + lift + swing).astype(jnp.int32)
    bounds = jnp.cumsum(loads)
    entries = jnp.arange(2 * TOK_DEV, dtype=jnp.int32)
    groups = jnp.sum((entries[:, None] >= bounds[None, :]).astype(jnp.int32), axis=1)
    paired = jnp.stack([groups[:TOK_DEV], groups[TOK_DEV:]], axis=1)
    shuffle = jax.random.permutation(key_rows, TOK_DEV)
    return paired[shuffle].astype(jnp.int32)


def draw_routes(key, part):
    key = jax.random.fold_in(key, 11)
    key_hot, key_blocks = jax.random.split(key)
    hottest = jax.random.randint(key_hot, (SECTIONS,), 0, EXPERTS)
    block_hot = jnp.repeat(hottest, OWNERS)
    block_keys = jax.random.split(key_blocks, SECTIONS * OWNERS)
    blocks = jax.vmap(route_block)(block_keys, block_hot)
    return blocks.reshape(SECTIONS, TOKENS, 2).astype(jnp.int32)


def draw_router_logits(key, part):
    key = jax.random.fold_in(key, 5)
    key_base = jax.random.fold_in(key, 0)
    shape = (SECTIONS, TOKENS, EXPERTS)
    values = 1.5 * jax.random.normal(key_base, shape, jnp.float32)
    return values


def steps_of(stream_key, extent, shards, least, high):
    loudness = 1.0
    for dim, shards_of in shards:
        draws = jax.random.uniform(jax.random.fold_in(jax.random.fold_in(stream_key, 6), dim), (shards_of,), jnp.float32, least / len(shards), high / len(shards))
        loudness = loudness * jnp.repeat(jnp.exp(draws), extent[dim] // shards_of).reshape((-1,) + (1,) * (len(extent) - 1 - dim))
    return loudness


def bell_draw(own_key, shape, spread, most, shards=(), held_as=jnp.bfloat16):
    values = jax.random.normal(own_key, shape, jnp.float32) * spread
    if len(shards) > 0:
        values = steps_of(own_key, shape, shards, -0.22, 0.18) * values
    return jnp.clip(values, min=-most, max=most).astype(held_as)


def setup_inputs(seed: int = 0) -> dict:
    seeds = jax.random.split(jax.random.key(seed), 6)
    return {
        "grad_codes": draw_grad_codes(jax.random.fold_in(seeds[5], 71), 0),
        "grad_scales": jnp.clip(jnp.exp(math.log(0.0099487305) - 2.2979944 * jax.random.uniform(seeds[1], (SECTIONS, TOKENS), jnp.float32) ** steps_of(seeds[1], (SECTIONS, TOKENS), ((0, 8), (1, 64)), -0.2, 0.2)), 0.0009994507, 0.0099487305).astype(jnp.bfloat16),
        "routes": draw_routes(jax.random.fold_in(seeds[5], 71), 0),
        "router_logits": draw_router_logits(jax.random.fold_in(seeds[5], 71), 0),
        "expert_outputs": bell_draw(seeds[4], (SECTIONS, OWNERS, OWNERS * CAP, DWQ), 0.2, 1.1953125, ((0, 8), (1, 64))),
    }


def section_logit_grad(quant_codes, quant_scales, chosen, logits, outputs):
    gradient = (quant_codes.astype(jnp.float32) * quant_scales.astype(jnp.float32)[:, None]).astype(jnp.bfloat16)
    expert_ids = jnp.arange(EXPERTS, dtype=jnp.int32)
    chosen_hit = (chosen[:, :, None] == expert_ids[None, None, :]).astype(jnp.int32)
    per_token = lax.optimization_barrier(jnp.sum(chosen_hit, axis=1))
    before = jnp.cumsum(per_token, axis=0) - per_token
    position = lax.optimization_barrier(jnp.sum(chosen_hit * before[:, None, :], axis=2)).astype(jnp.int32)
    replicas = OWNERS // EXPERTS
    whole_rows = outputs.reshape(EXPERTS, replicas, OWNERS * CAP, DWQ)
    whole_rows = jnp.transpose(whole_rows, (0, 2, 1, 3)).reshape(EXPERTS, OWNERS * CAP, DW)
    saved_rows = whole_rows[chosen, position]
    gate_grad = jnp.einsum('tf,tcf->tc', gradient.astype(jnp.float32), saved_rows.astype(jnp.float32))
    gate_terms = lax.optimization_barrier(jnp.sum(chosen_hit.astype(jnp.float32) * gate_grad[:, :, None], axis=1))
    router_probs = jax.nn.softmax(logits, axis=-1)
    return router_probs * (gate_terms - lax.optimization_barrier(jnp.sum(router_probs * gate_terms, axis=-1, keepdims=True)))

def reference(grad_codes, grad_scales, routes, router_logits, expert_outputs):
    incoming_codes = jnp.roll(grad_codes, -1, axis=0)
    incoming_scales = jnp.roll(grad_scales, -1, axis=0)
    return lax.map(lambda item: section_logit_grad(*item), (incoming_codes, incoming_scales, routes, router_logits, expert_outputs))
```

```python
import functools

import jax
import jax.numpy as jnp
from jax import lax
from jax.experimental import pallas as pl
from jax.experimental.pallas import tpu as pltpu
from jax.sharding import PartitionSpec as P

ROWS = 8
COLS = 8
NEAR = (1, -1, 2, -2, 3, -3, 0)
WIDE = 2
META = 16
VMEM = pl.BlockSpec(memory_space=pltpu.VMEM)
SMEM = pl.BlockSpec(memory_space=pltpu.SMEM)
ANY = pl.BlockSpec(memory_space=pl.ANY)


def along_section(x, by):
    n = lax.axis_size("section")
    return lax.ppermute(x, "section", [(i, (i + by) % n) for i in range(n)])


def along_y(x, by):
    return lax.ppermute(
        x, "expert", [(i, (i + COLS * by) % (ROWS * COLS)) for i in range(ROWS * COLS)]
    )


def along_z(x, step):
    return lax.ppermute(
        x,
        "expert",
        [(i, (i // COLS) * COLS + (i + step(i % COLS)) % COLS) for i in range(ROWS * COLS)],
    )


def exchange_z(x):
    groups = [[y * COLS + z for z in range(COLS)] for y in range(ROWS)]
    return lax.all_to_all(
        x, "expert", split_axis=0, concat_axis=0, axis_index_groups=groups, tiled=True
    )


def two_away(z):
    return 2 if z % 2 == 0 else -2


def wrap(i, n):
    return lax.rem(i + n, n)


def call(kernel, out_shape, specs, cost=1, **kw):
    return pl.pallas_call(
        kernel,
        out_shape=out_shape,
        in_specs=specs,
        out_specs=jax.tree.map(lambda _: VMEM, out_shape),
        compiler_params=pltpu.CompilerParams(vmem_limit_bytes=16 * 1024 * 1024),
        cost_estimate=pl.CostEstimate(flops=cost, bytes_accessed=1 << 20, transcendentals=0),
        **kw,
    )


def slab_kernel(cap, steps, counts_ref, place_ref, saved_ref, *refs):
    n = len(steps)
    outs, (offsets, windows, slabs, reads, writes) = refs[:n], refs[n:]
    total = saved_ref.shape[0]
    slab = cap * COLS
    reach = slab + 16
    y = place_ref[0] // COLS

    def add(i, before):
        offsets[i] = before
        return before + counts_ref[i]

    lax.fori_loop(0, ROWS * COLS, add, jnp.int32(0))
    rows = [wrap(y + by, ROWS) for by in steps]
    bases = [
        pl.multiple_of(jnp.minimum((offsets[r * COLS] // 16) * 16, total - reach), 16) for r in rows
    ]
    fetch = [
        pltpu.make_async_copy(saved_ref.at[pl.ds(bases[k], reach)], windows.at[k], reads.at[k])
        for k in range(n)
    ]
    store = [pltpu.make_async_copy(slabs.at[k], outs[k], writes.at[k]) for k in range(n)]
    for f in fetch:
        f.start()
    line = lax.broadcasted_iota(jnp.int32, (slab, reach), 0)
    lane = lax.broadcasted_iota(jnp.int32, (slab, reach), 1)
    for k, by in enumerate(steps):
        if by == 4:
            at = jnp.zeros((slab, reach), jnp.int32)
            for c in range(COLS):
                shift = offsets[rows[k] * COLS + c] - bases[k] - c * cap
                at = jnp.where((line >= c * cap) & (line < (c + 1) * cap), line + shift, at)
        else:
            at = line + (offsets[rows[k] * COLS] - bases[k])
        fetch[k].wait()
        slabs[k] = jnp.dot(
            (lane == at).astype(jnp.bfloat16), windows[k], preferred_element_type=jnp.float32
        ).astype(jnp.bfloat16)
        store[k].start()
    for w in store:
        w.wait()


def cut_slabs(cap, steps, counts, place, saved):
    slab, width = cap * COLS, saved.shape[1]
    n = len(steps)
    return pl.pallas_call(
        functools.partial(slab_kernel, cap, steps),
        out_shape=[jax.ShapeDtypeStruct((slab, width), saved.dtype)] * n,
        in_specs=[SMEM, SMEM, ANY],
        out_specs=[ANY] * n,
        scratch_shapes=[
            pltpu.SMEM((ROWS * COLS,), jnp.int32),
            pltpu.VMEM((n, slab + 16, width), saved.dtype),
            pltpu.VMEM((n, slab, width), saved.dtype),
            pltpu.SemaphoreType.DMA((n,)),
            pltpu.SemaphoreType.DMA((n,)),
        ],
        compiler_params=pltpu.CompilerParams(vmem_limit_bytes=16 * 1024 * 1024),
        cost_estimate=pl.CostEstimate(
            flops=n * 2 * slab * (slab + 16) * width,
            bytes_accessed=n * 4 * slab * width,
            transcendentals=0,
        ),
    )(counts, place, saved)


def payload_kernel(place_ref, codes_ref, meta_ref, own_ref, up_ref, down_ref, two_ref):
    z = wrap(place_ref[0], COLS)
    quarter = own_ref.shape[0] - META
    for by, out in ((0, own_ref), (1, up_ref), (3, down_ref), (2, two_ref)):
        q = lax.rem(z + by, 4)
        part = codes_ref[:, pl.ds(pl.multiple_of(q * quarter, quarter), quarter)]
        out[:quarter] = part.T
        out[quarter:] = meta_ref[...]


def gather_kernel(*refs):
    blocks, out_ref = refs[:-1], refs[-1]
    tokens = blocks[0].shape[1]
    for j, block in enumerate(blocks):
        out_ref[:, j * tokens : (j + 1) * tokens] = block[...]


def columns_of(z):
    odd = lax.rem(z, 2) == 1
    two = jnp.where(odd, z + 2, z - 2)
    return [
        lax.rem(c + 2 * COLS, COLS)
        for c in (z, z - 1, z + 1, two, z + 4, z + 3, z + 5, two + 4)
    ]


def meet_kernel(steps, place_ref, first_ref, second_ref, *refs):
    slabs, out_ref = refs[:-1], refs[-1]
    slab = slabs[0].shape[0]
    tokens = out_ref.shape[2]
    y = place_ref[0] // COLS
    z = lax.rem(place_ref[0], COLS)
    half = z // 4
    column = columns_of(z)
    quarter = first_ref.shape[0] - META
    k_of = lax.broadcasted_iota(jnp.int32, (8, 1), 0)
    expert = jnp.full((8, 1), -1, jnp.int32)
    for k, by in enumerate(steps):
        expert = jnp.where(k_of == k, 2 * wrap(y - by, ROWS) + half, expert)
    expert = expert.astype(jnp.float32)
    notes = [r[quarter:].astype(jnp.float32) for r in (first_ref, second_ref)]

    def note(i, j):
        return notes[j // 4][i : i + 1, (j % 4) * tokens : (j % 4 + 1) * tokens]

    hits = [[note(i, j) == expert for i in range(2)] for j in range(8)]
    loads = [
        jnp.sum((h[0] | h[1]).astype(jnp.float32), axis=1, keepdims=True) for h in hits
    ]
    wants = []
    for j in range(8):
        base = jnp.zeros((8, 1), jnp.float32)
        for i in range(8):
            if i != j:
                base = base + jnp.where(column[i] < column[j], loads[i], 0.0)
        wants.append(
            jnp.where(hits[j][0], note(2, j) + base, jnp.where(hits[j][1], note(3, j) + base, -1.0))
        )
    line = lax.broadcasted_iota(jnp.int32, (slab, tokens), 0).astype(jnp.float32)
    rows = [[] for _ in range(8)]
    for k, slab_ref in enumerate(slabs):
        for g, codes_ref in enumerate((first_ref, second_ref)):
            scores = jnp.dot(
                slab_ref[...], codes_ref[:quarter], preferred_element_type=jnp.float32
            )
            for j in range(4):
                mask = line == wants[g * 4 + j][k : k + 1]
                picked = jnp.where(mask, scores[:, j * tokens : (j + 1) * tokens], 0.0)
                rows[g * 4 + j].append(jnp.sum(picked, axis=0, keepdims=True))
    for j in range(8):
        out_ref[column[j]] = jnp.concatenate(rows[j], axis=0)


def finish_kernel(
    cap, place_ref, back_ref, direct_ref, codes_ref, meta_ref, scales_ref, logits_ref, out_ref, gate_ref
):
    tokens = codes_ref.shape[0]
    quarter = direct_ref.shape[1]
    y = place_ref[0] // COLS
    meta = meta_ref[...].astype(jnp.float32)
    named, slots = [meta[0:1], meta[1:2]], [meta[2:3], meta[3:4]]
    scores = [
        lax.dot_general(
            direct_ref[...], codes_ref[:, q * quarter : (q + 1) * quarter],
            (((1,), (1,)), ((), ())), preferred_element_type=jnp.float32,
        )
        for q in range(4)
    ]
    line = lax.broadcasted_iota(jnp.int32, (cap, tokens), 0).astype(jnp.float32)
    for half in range(2):
        sums = back_ref[half * 4]
        for q in range(1, 4):
            sums = sums + back_ref[half * 4 + q]
        for k, by in enumerate(NEAR):
            gate_ref[pl.ds(2 * wrap(y - by, ROWS) + half, 1)] = sums[k : k + 1]
        far = 2 * wrap(y + 4, ROWS) + half
        far_f = far.astype(jnp.float32)
        want = jnp.where(named[0] == far_f, slots[0], jnp.where(named[1] == far_f, slots[1], -1.0))
        total = jnp.zeros((cap, tokens), jnp.float32)
        for q in range(4):
            at = (half * 4 + q) * cap
            total = total + scores[q][at : at + cap]
        gate_ref[pl.ds(far, 1)] = jnp.sum(
            jnp.where(line == want, total, 0.0), axis=0, keepdims=True
        )
    gate = gate_ref[...] * scales_ref[...]
    logits = logits_ref[...]
    powers = jnp.exp(logits - jnp.max(logits, axis=0, keepdims=True))
    probs = powers / jnp.sum(powers, axis=0, keepdims=True)
    out_ref[...] = probs * (gate - jnp.sum(probs * gate, axis=0, keepdims=True))


def local(grad_codes, grad_scales, routes, router_logits, expert_outputs):
    codes, scales = along_section(grad_codes[0], -1), along_section(grad_scales[0], -1)
    saved = expert_outputs[0, 0]
    place = lax.axis_index("expert").astype(jnp.int32)[None]
    cap = saved.shape[0] // (ROWS * COLS)
    slab = cap * COLS
    quarter = saved.shape[1]
    tokens = codes.shape[0]
    experts = router_logits.shape[2]
    bf16, f32 = jnp.bfloat16, jnp.float32

    chosen = routes[0].T
    ids = jnp.arange(experts, dtype=jnp.int32)
    hits = [(chosen[c][None] == ids[:, None]).astype(f32) for c in range(2)]
    counts = jnp.sum(hits[0] + hits[1], axis=1)
    load = lax.all_to_all(
        jnp.broadcast_to(jnp.repeat(counts, 4)[:, None, None].astype(jnp.int32), (64, WIDE, 128)),
        "expert", split_axis=0, concat_axis=0, tiled=True,
    )[:, 0, 0]

    upper = (jnp.arange(tokens)[:, None] < jnp.arange(tokens)[None]).astype(f32)
    before = jnp.dot(hits[0] + hits[1], upper)
    slots = [jnp.sum(h * before, axis=0) for h in hits]
    meta = jnp.stack([chosen[0].astype(f32), chosen[1].astype(f32)] + slots)
    meta = jnp.pad(meta, ((0, META - 4), (0, 0))).astype(bf16)

    block = jax.ShapeDtypeStruct((quarter + META, tokens), bf16)
    own, up, down, two = call(payload_kernel, [block] * 4, [SMEM, VMEM, VMEM])(place, codes, meta)
    up = along_z(up, lambda z: 1)
    down = along_z(down, lambda z: -1)
    two = along_z(two, two_away)

    ready, own = lax.optimization_barrier((place, own))
    *mine, pieces = cut_slabs(cap, (1, -1, 4), load, ready, saved)
    ready, mine[0] = lax.optimization_barrier((ready, mine[0]))
    mine = mine + list(cut_slabs(cap, (2, -2, 3, -3, 0), load, ready, saved))
    arrived = [along_y(mine[k], NEAR[k]) for k in range(4)]
    for k in (4, 5):
        payload, arrived[k - 4] = lax.optimization_barrier((mine[k], arrived[k - 4]))
        arrived.append(along_y(payload, NEAR[k]))
    arrived.append(mine[6])
    far, arrived[2] = lax.optimization_barrier(
        (exchange_z(pieces.reshape(COLS, cap, quarter)).reshape(slab, quarter), arrived[2])
    )
    direct = along_y(far, 4)

    own, arrived[6] = lax.optimization_barrier((own, arrived[6]))
    first = call(
        gather_kernel, jax.ShapeDtypeStruct((quarter + META, 4 * tokens), bf16), [VMEM] * 4
    )(own, up, down, two)
    second = along_z(first, lambda z: 4)

    def meet(steps, slabs):
        return call(
            functools.partial(meet_kernel, steps),
            jax.ShapeDtypeStruct((COLS, len(steps), tokens), f32), [SMEM] + [VMEM] * (2 + len(steps)),
            cost=2 * len(steps) * slab * quarter * COLS * tokens,
        )(place, first, second, *slabs)

    parts = jnp.concatenate([meet(NEAR, arrived), jnp.zeros((COLS, 1, tokens), f32)], axis=1)
    returned = exchange_z(parts)
    logit_grad = call(
        functools.partial(finish_kernel, cap),
        jax.ShapeDtypeStruct((experts, tokens), f32), [SMEM] + [VMEM] * 6,
        scratch_shapes=[pltpu.VMEM((experts, tokens), f32)],
    )(place, returned, direct, codes, meta, scales.astype(f32)[None], router_logits[0].T)
    return logit_grad.T[None]


def solution(mesh):
    placed = (
        P("section", "expert", None),
        P("section", "expert"),
        P("section", "expert", None),
        P("section", "expert", None),
        P("section", "expert", None, None),
    )
    return jax.shard_map(
        local, mesh=mesh, in_specs=placed, out_specs=P("section", "expert", None), check_vma=False
    )
```

```python
import functools

import jax
import jax.numpy as jnp
from jax import lax
from jax.experimental import pallas as pl
from jax.experimental.pallas import tpu as pltpu
from jax.sharding import PartitionSpec as P

ROWS = 8
COLS = 8
PARTS = 4
WIDE = 2
LANES = 128
VMEM = pl.BlockSpec(memory_space=pltpu.VMEM)
SMEM = pl.BlockSpec(memory_space=pltpu.SMEM)
HBM = pl.BlockSpec(memory_space=pltpu.HBM)


def along_section(x, by):
    n = lax.axis_size("section")
    return lax.ppermute(x, "section", [(i, (i + by) % n) for i in range(n)])


def exchange(x):
    devices = ROWS * COLS
    order = [i * PARTS + q for q in range(PARTS) for i in range(devices // PARTS)]
    return lax.all_to_all(
        x, "expert", split_axis=0, concat_axis=0, axis_index_groups=[order], tiled=True
    )


def call(kernel, out_shape, in_specs, out_specs=None, flops=0, mib=1, **kw):
    return pl.pallas_call(
        kernel,
        out_shape=out_shape,
        in_specs=in_specs,
        out_specs=jax.tree.map(lambda _: VMEM, out_shape) if out_specs is None else out_specs,
        compiler_params=pltpu.CompilerParams(vmem_limit_bytes=60 * 1024 * 1024),
        cost_estimate=pl.CostEstimate(flops=flops, bytes_accessed=mib << 20, transcendentals=0),
        **kw,
    )


def count_kernel(routes_ref, out_ref):
    experts = out_ref.shape[0] // PARTS
    ids = lax.broadcasted_iota(jnp.int32, (experts, LANES), 0)
    hit = (routes_ref[0:1] == ids) | (routes_ref[1:2] == ids)
    counts = jnp.sum(hit.astype(jnp.int32), axis=1, keepdims=True)
    for o in range(out_ref.shape[0]):
        out_ref[o] = jnp.broadcast_to(counts[o // PARTS : o // PARTS + 1], (WIDE, LANES))


def slab_kernel(cap, counts_ref, saved_ref, out_ref, windows, wide, slabs, reads, writes):
    devices = ROWS * COLS
    total, reach, tail = saved_ref.shape[0], windows.shape[1], wide.shape[2]
    counts = counts_ref[:, 0].astype(jnp.float32)
    earlier = lax.broadcasted_iota(jnp.int32, (devices, devices), 1) < lax.broadcasted_iota(
        jnp.int32, (devices, devices), 0
    )
    offsets = jnp.dot(
        earlier.astype(jnp.float32), counts, preferred_element_type=jnp.float32,
        precision=lax.Precision.HIGHEST,
    ).astype(jnp.int32)
    at = [jnp.max(offsets[d : d + 1]) for d in range(devices)]
    bases, fetch = [], []
    for r in range(ROWS):
        base = jnp.minimum((at[r * COLS] // 16) * 16, total - reach)
        bases.append(pl.multiple_of(base, 16))
        fetch.append(
            pltpu.make_async_copy(
                saved_ref.at[pl.ds(bases[r], reach)], windows.at[r], reads.at[r]
            )
        )
        fetch[r].start()
    for b in range(2):
        wide[b, :, reach:] = jnp.zeros((wide.shape[1], tail - reach, LANES), jnp.float32)
    two = 2 * cap
    store = [
        pltpu.make_async_copy(
            slabs.at[:, pl.ds(r * two, two)], out_ref.at[:, pl.ds(r * two, two)], writes.at[r]
        )
        for r in range(ROWS)
    ]
    for r in range(ROWS):
        b = r % 2
        fetch[r].wait()
        for k in range(wide.shape[1]):
            wide[b, k, :reach] = windows[r, :, k * LANES : (k + 1) * LANES].astype(jnp.float32)
        for k in range(wide.shape[1]):
            for q in range(PARTS):
                rows = [
                    wide[b, k, pl.ds(at[r * COLS + c] - bases[r], cap), :]
                    for c in (q, q + PARTS)
                ]
                slabs[q, r * two : (r + 1) * two, k * LANES : (k + 1) * LANES] = jnp.concatenate(
                    rows, axis=0
                ).astype(jnp.bfloat16)
        store[r].start()
    for w in store:
        w.wait()


def finish_kernel(cap, routes_ref, scales_ref, logits_ref, codes_ref, rows_ref, out_ref, rows, sems):
    experts, tokens = logits_ref.shape
    quarter = rows.shape[2]
    fetch = [pltpu.make_async_copy(rows_ref.at[q], rows.at[q], sems.at[q]) for q in range(PARTS)]
    for f in fetch:
        f.start()
    ids = lax.broadcasted_iota(jnp.int32, (experts, tokens), 0)
    hit = (routes_ref[0:1] == ids) | (routes_ref[1:2] == ids)
    upper = lax.broadcasted_iota(jnp.int32, (tokens, tokens), 0) < lax.broadcasted_iota(
        jnp.int32, (tokens, tokens), 1
    )
    before = jnp.dot(
        hit.astype(jnp.float32), upper.astype(jnp.float32), preferred_element_type=jnp.float32
    )
    want = jnp.where(hit, before, -1.0)
    logits = logits_ref[...]
    powers = jnp.exp(logits - jnp.max(logits, axis=0, keepdims=True))
    probs = powers / jnp.sum(powers, axis=0, keepdims=True)
    scores = jnp.zeros((experts * cap, tokens), jnp.float32)
    for q in range(PARTS):
        fetch[q].wait()
        scores = scores + lax.dot_general(
            rows[q], codes_ref[:, q * quarter : (q + 1) * quarter], (((1,), (1,)), ((), ())),
            preferred_element_type=jnp.float32,
        )
    line = lax.broadcasted_iota(jnp.int32, (cap, tokens), 0).astype(jnp.float32)
    gate = jnp.concatenate(
        [
            jnp.sum(
                jnp.where(line == want[e : e + 1], scores[e * cap : (e + 1) * cap], 0.0),
                axis=0, keepdims=True,
            )
            for e in range(experts)
        ],
        axis=0,
    )
    gate = gate * scales_ref[...]
    out_ref[...] = probs * (gate - jnp.sum(probs * gate, axis=0, keepdims=True))


def local(grad_codes, grad_scales, routes, router_logits, expert_outputs):
    codes, scales = along_section(grad_codes[0], -1), along_section(grad_scales[0], -1)
    saved = expert_outputs[0, 0]
    devices = ROWS * COLS
    cap = saved.shape[0] // devices
    slab = cap * COLS
    quarter = saved.shape[1]
    tokens = codes.shape[0]
    experts = router_logits.shape[2]
    bf16, f32 = jnp.bfloat16, jnp.float32
    shape, dma = jax.ShapeDtypeStruct, pltpu.SemaphoreType.DMA

    chosen = routes[0].T
    load = lax.all_to_all(
        call(count_kernel, shape((devices, WIDE, LANES), jnp.int32), [VMEM])(chosen),
        "expert", split_axis=0, concat_axis=0, tiled=True,
    )
    mine = call(
        functools.partial(slab_kernel, cap), shape((PARTS, experts * cap, quarter), bf16),
        [VMEM, HBM], HBM, mib=6,
        scratch_shapes=[
            pltpu.VMEM((ROWS, slab + 16, quarter), bf16),
            pltpu.VMEM((2, quarter // LANES, slab + 16 + cap, LANES), f32),
            pltpu.VMEM((PARTS, experts * cap, quarter), bf16),
            dma((ROWS,)), dma((ROWS,)),
        ],
    )(load, saved)
    rows = exchange(mine.reshape(devices, cap, quarter)).reshape(PARTS, experts * cap, quarter)
    logit_grad = call(
        functools.partial(finish_kernel, cap), shape((experts, tokens), f32), [VMEM] * 4 + [HBM],
        scratch_shapes=[pltpu.VMEM((PARTS, experts * cap, quarter), bf16), dma((PARTS,))],
    )(chosen, scales.astype(f32)[None], router_logits[0].T, codes, rows)
    return logit_grad.T[None]


def solution(mesh):
    placed = (
        P("section", "expert", None),
        P("section", "expert"),
        P("section", "expert", None),
        P("section", "expert", None),
        P("section", "expert", None, None),
    )
    return jax.shard_map(
        local, mesh=mesh, in_specs=placed, out_specs=P("section", "expert", None), check_vma=False
    )
```

```python
import functools

import jax
import jax.numpy as jnp
from jax import lax
from jax.experimental import pallas as pl
from jax.experimental.pallas import tpu as pltpu
from jax.sharding import PartitionSpec as P

ROWS = 8
COLS = 8
PARTS = 4
WIDE = 1
LANES = 128
VMEM = pl.BlockSpec(memory_space=pltpu.VMEM)
SMEM = pl.BlockSpec(memory_space=pltpu.SMEM)
HBM = pl.BlockSpec(memory_space=pltpu.HBM)


def along_section(x, by):
    n = lax.axis_size("section")
    return lax.ppermute(x, "section", [(i, (i + by) % n) for i in range(n)])


def exchange(x):
    devices = ROWS * COLS
    order = [i * PARTS + q for q in range(PARTS) for i in range(devices // PARTS)]
    return lax.all_to_all(
        x, "expert", split_axis=0, concat_axis=0, axis_index_groups=[order], tiled=True
    )


def call(kernel, out_shape, in_specs, out_specs=None, flops=0, mib=1, vmem=60, **kw):
    return pl.pallas_call(
        kernel,
        out_shape=out_shape,
        in_specs=in_specs,
        out_specs=jax.tree.map(lambda _: VMEM, out_shape) if out_specs is None else out_specs,
        compiler_params=pltpu.CompilerParams(vmem_limit_bytes=vmem << 20),
        cost_estimate=pl.CostEstimate(flops=flops, bytes_accessed=mib << 20, transcendentals=0),
        **kw,
    )


def count_kernel(routes_ref, out_ref):
    experts = out_ref.shape[0] // PARTS
    ids = lax.broadcasted_iota(jnp.int32, (experts, LANES), 0)
    hit = (routes_ref[0:1] == ids) | (routes_ref[1:2] == ids)
    counts = jnp.sum(hit.astype(jnp.int32), axis=1, keepdims=True)
    for o in range(out_ref.shape[0]):
        out_ref[o] = jnp.broadcast_to(counts[o // PARTS : o // PARTS + 1], (WIDE, LANES))


def slab_kernel(cap, counts_ref, saved_ref, out_ref, windows, wide, slabs, reads, writes):
    devices = ROWS * COLS
    total, reach, tail = saved_ref.shape[0], windows.shape[1], wide.shape[2]
    counts = counts_ref[:, 0].astype(jnp.float32)
    earlier = lax.broadcasted_iota(jnp.int32, (devices, devices), 1) < lax.broadcasted_iota(
        jnp.int32, (devices, devices), 0
    )
    offsets = jnp.dot(
        earlier.astype(jnp.bfloat16), counts.astype(jnp.bfloat16),
        preferred_element_type=jnp.float32,
    ).astype(jnp.int32)
    at = [offsets[d, 0] for d in range(devices)]
    bases, fetch = [], []
    for r in range(ROWS):
        base = jnp.minimum((at[r * COLS] // 16) * 16, total - reach)
        bases.append(pl.multiple_of(base, 16))
        fetch.append(
            pltpu.make_async_copy(
                saved_ref.at[pl.ds(bases[r], reach)], windows.at[r], reads.at[r]
            )
        )
        fetch[r].start()
    for b in range(2):
        wide[b, :, reach:] = jnp.zeros((wide.shape[1], tail - reach, LANES), jnp.float32)
    two = 2 * cap
    store = [
        pltpu.make_async_copy(
            slabs.at[:, pl.ds(r * two, two)], out_ref.at[:, pl.ds(r * two, two)], writes.at[r]
        )
        for r in range(ROWS)
    ]
    for r in range(ROWS):
        b = r % 2
        fetch[r].wait()
        for k in range(wide.shape[1]):
            wide[b, k, :reach] = windows[r, :, k * LANES : (k + 1) * LANES].astype(jnp.float32)
        for k in range(wide.shape[1]):
            for q in range(PARTS):
                rows = [
                    wide[b, k, pl.ds(at[r * COLS + c] - bases[r], cap), :]
                    for c in (q, q + PARTS)
                ]
                slabs[q, r * two : (r + 1) * two, k * LANES : (k + 1) * LANES] = jnp.concatenate(
                    rows, axis=0
                ).astype(jnp.bfloat16)
        store[r].start()
    for w in store:
        w.wait()


def finish_kernel(cap, routes_ref, scales_ref, logits_ref, codes_ref, rows, out_ref):
    experts, tokens = logits_ref.shape
    quarter = rows.shape[2]
    ids = lax.broadcasted_iota(jnp.int32, (experts, tokens), 0)
    hit = (routes_ref[0:1] == ids) | (routes_ref[1:2] == ids)
    upper = lax.broadcasted_iota(jnp.int32, (tokens, tokens), 0) < lax.broadcasted_iota(
        jnp.int32, (tokens, tokens), 1
    )
    before = jnp.dot(
        hit.astype(jnp.float32), upper.astype(jnp.float32), preferred_element_type=jnp.float32
    )
    want = jnp.where(hit, before, -1.0)
    logits = logits_ref[...]
    powers = jnp.exp(logits - jnp.max(logits, axis=0, keepdims=True))
    probs = powers / jnp.sum(powers, axis=0, keepdims=True)
    scores = jnp.zeros((experts * cap, tokens), jnp.float32)
    for q in range(PARTS):
        scores = scores + lax.dot_general(
            rows[q], codes_ref[:, q * quarter : (q + 1) * quarter], (((1,), (1,)), ((), ())),
            preferred_element_type=jnp.float32,
        )
    line = lax.broadcasted_iota(jnp.int32, (cap, tokens), 0).astype(jnp.float32)
    gate = jnp.concatenate(
        [
            jnp.sum(
                jnp.where(line == want[e : e + 1], scores[e * cap : (e + 1) * cap], 0.0),
                axis=0, keepdims=True,
            )
            for e in range(experts)
        ],
        axis=0,
    )
    gate = gate * scales_ref[...]
    out_ref[...] = probs * (gate - jnp.sum(probs * gate, axis=0, keepdims=True))


def local(grad_codes, grad_scales, routes, router_logits, expert_outputs):
    codes, scales = along_section(grad_codes[0], -1), along_section(grad_scales[0], -1)
    saved = expert_outputs[0, 0]
    devices = ROWS * COLS
    cap = saved.shape[0] // devices
    slab = cap * COLS
    quarter = saved.shape[1]
    tokens = codes.shape[0]
    experts = router_logits.shape[2]
    bf16, f32 = jnp.bfloat16, jnp.float32
    shape, dma = jax.ShapeDtypeStruct, pltpu.SemaphoreType.DMA

    chosen = routes[0].T
    load = lax.all_to_all(
        call(count_kernel, shape((devices, WIDE, LANES), jnp.int32), [VMEM])(chosen),
        "expert", split_axis=0, concat_axis=0, tiled=True,
    )
    mine = call(
        functools.partial(slab_kernel, cap), shape((PARTS, experts * cap, quarter), bf16),
        [VMEM, HBM], HBM, mib=6,
        scratch_shapes=[
            pltpu.VMEM((ROWS, slab + 16, quarter), bf16),
            pltpu.VMEM((2, quarter // LANES, slab + 16 + cap, LANES), f32),
            pltpu.VMEM((PARTS, experts * cap, quarter), bf16),
            dma((ROWS,)), dma((ROWS,)),
        ],
    )(load, saved)
    rows = exchange(mine.reshape(devices, cap, quarter)).reshape(PARTS, experts * cap, quarter)
    logit_grad = call(
        functools.partial(finish_kernel, cap), shape((experts, tokens), f32), [VMEM] * 5, vmem=16,
    )(chosen, scales.astype(f32)[None], router_logits[0].T, codes, rows)
    return logit_grad.T[None]


def solution(mesh):
    placed = (
        P("section", "expert", None),
        P("section", "expert"),
        P("section", "expert", None),
        P("section", "expert", None),
        P("section", "expert", None, None),
    )
    return jax.shard_map(
        local, mesh=mesh, in_specs=placed, out_specs=P("section", "expert", None), check_vma=False
    )
```

```python
import functools

import jax
import jax.numpy as jnp
from jax import lax
from jax.experimental import pallas as pl
from jax.experimental.pallas import tpu as pltpu
from jax.sharding import PartitionSpec as P

ROWS = 8
COLS = 8
PARTS = 4
WIDE = 1
LANES = 128
VMEM = pl.BlockSpec(memory_space=pltpu.VMEM)
SMEM = pl.BlockSpec(memory_space=pltpu.SMEM)
HBM = pl.BlockSpec(memory_space=pltpu.HBM)


def along_section(x, by):
    n = lax.axis_size("section")
    return lax.ppermute(x, "section", [(i, (i + by) % n) for i in range(n)])


def exchange(x):
    devices = ROWS * COLS
    order = [i * PARTS + q for q in range(PARTS) for i in range(devices // PARTS)]
    return lax.all_to_all(
        x, "expert", split_axis=0, concat_axis=0, axis_index_groups=[order], tiled=True
    )


def call(kernel, out_shape, in_specs, out_specs=None, flops=0, mib=1, vmem=60, **kw):
    return pl.pallas_call(
        kernel,
        out_shape=out_shape,
        in_specs=in_specs,
        out_specs=jax.tree.map(lambda _: VMEM, out_shape) if out_specs is None else out_specs,
        compiler_params=pltpu.CompilerParams(vmem_limit_bytes=vmem << 20),
        cost_estimate=pl.CostEstimate(flops=flops, bytes_accessed=mib << 20, transcendentals=0),
        **kw,
    )


def count_kernel(routes_ref, out_ref):
    experts = out_ref.shape[0] // PARTS
    ids = lax.broadcasted_iota(jnp.int32, (experts, LANES), 0)
    hit = (routes_ref[0:1] == ids) | (routes_ref[1:2] == ids)
    counts = jnp.sum(hit.astype(jnp.int32), axis=1, keepdims=True)
    for o in range(out_ref.shape[0]):
        out_ref[o] = jnp.broadcast_to(counts[o // PARTS : o // PARTS + 1], (WIDE, LANES))


def slab_kernel(cap, counts_ref, saved_ref, out_ref, held, counts_vmem, wide, slabs, reads, writes):
    devices = ROWS * COLS
    total, tail = saved_ref.shape[0], wide.shape[2]
    reach, depth = tail - cap, total // ROWS
    first = pltpu.make_async_copy(counts_ref, counts_vmem, reads.at[ROWS])
    first.start()
    fetch = [
        pltpu.make_async_copy(
            saved_ref.at[pl.ds(r * depth, depth)], held.at[pl.ds(r * depth, depth)], reads.at[r]
        )
        for r in range(ROWS)
    ]
    for f in fetch:
        f.start()
    first.wait()
    counts = counts_vmem[:, 0].astype(jnp.float32)
    earlier = lax.broadcasted_iota(jnp.int32, (devices, devices), 1) < lax.broadcasted_iota(
        jnp.int32, (devices, devices), 0
    )
    offsets = jnp.dot(
        earlier.astype(jnp.bfloat16), counts.astype(jnp.bfloat16),
        preferred_element_type=jnp.float32,
    ).astype(jnp.int32)
    at = [offsets[d, 0] for d in range(devices)]
    bases = [
        pl.multiple_of(jnp.minimum((at[r * COLS] // 16) * 16, total - reach), 16)
        for r in range(ROWS)
    ]
    for b in range(2):
        wide[b, :, reach:] = jnp.zeros((wide.shape[1], tail - reach, LANES), jnp.float32)
    two = 2 * cap
    store = [
        pltpu.make_async_copy(
            slabs.at[:, pl.ds(r * two, two)], out_ref.at[:, pl.ds(r * two, two)], writes.at[r]
        )
        for r in range(ROWS)
    ]
    for r in range(ROWS):
        b = r % 2
        for f in fetch[:2] if r == 0 else fetch[r + 1 : r + 2]:
            f.wait()
        for k in range(wide.shape[1]):
            wide[b, k, :reach] = held[
                pl.ds(bases[r], reach), k * LANES : (k + 1) * LANES
            ].astype(jnp.float32)
        for k in range(wide.shape[1]):
            for q in range(PARTS):
                rows = [
                    wide[b, k, pl.ds(at[r * COLS + c] - bases[r], cap), :]
                    for c in (q, q + PARTS)
                ]
                slabs[q, r * two : (r + 1) * two, k * LANES : (k + 1) * LANES] = jnp.concatenate(
                    rows, axis=0
                ).astype(jnp.bfloat16)
        store[r].start()
    for w in store:
        w.wait()


def finish_kernel(cap, routes_ref, scales_ref, logits_ref, codes_ref, rows, out_ref):
    experts, tokens = logits_ref.shape
    quarter = rows.shape[2]
    ids = lax.broadcasted_iota(jnp.int32, (experts, tokens), 0)
    hit = (routes_ref[0:1] == ids) | (routes_ref[1:2] == ids)
    upper = lax.broadcasted_iota(jnp.int32, (tokens, tokens), 0) < lax.broadcasted_iota(
        jnp.int32, (tokens, tokens), 1
    )
    before = jnp.dot(
        hit.astype(jnp.float32), upper.astype(jnp.float32), preferred_element_type=jnp.float32
    )
    want = jnp.where(hit, before, -1.0)
    logits = logits_ref[...]
    powers = jnp.exp(logits - jnp.max(logits, axis=0, keepdims=True))
    probs = powers / jnp.sum(powers, axis=0, keepdims=True)
    scores = jnp.zeros((experts * cap, tokens), jnp.float32)
    for q in range(PARTS):
        scores = scores + lax.dot_general(
            rows[q], codes_ref[:, q * quarter : (q + 1) * quarter], (((1,), (1,)), ((), ())),
            preferred_element_type=jnp.float32,
        )
    line = lax.broadcasted_iota(jnp.int32, (cap, tokens), 0).astype(jnp.float32)
    gate = jnp.concatenate(
        [
            jnp.sum(
                jnp.where(line == want[e : e + 1], scores[e * cap : (e + 1) * cap], 0.0),
                axis=0, keepdims=True,
            )
            for e in range(experts)
        ],
        axis=0,
    )
    gate = gate * scales_ref[...]
    out_ref[...] = probs * (gate - jnp.sum(probs * gate, axis=0, keepdims=True))


def local(grad_codes, grad_scales, routes, router_logits, expert_outputs):
    codes, scales = along_section(grad_codes[0], -1), along_section(grad_scales[0], -1)
    saved = expert_outputs[0, 0]
    devices = ROWS * COLS
    cap = saved.shape[0] // devices
    slab = cap * COLS
    quarter = saved.shape[1]
    tokens = codes.shape[0]
    experts = router_logits.shape[2]
    bf16, f32 = jnp.bfloat16, jnp.float32
    shape, dma = jax.ShapeDtypeStruct, pltpu.SemaphoreType.DMA

    chosen = routes[0].T
    load = lax.all_to_all(
        call(count_kernel, shape((devices, WIDE, LANES), jnp.int32), [VMEM])(chosen),
        "expert", split_axis=0, concat_axis=0, tiled=True,
    )
    mine = call(
        functools.partial(slab_kernel, cap), shape((PARTS, experts * cap, quarter), bf16),
        [HBM, HBM], HBM, mib=6,
        scratch_shapes=[
            pltpu.VMEM(saved.shape, bf16),
            pltpu.VMEM((devices, WIDE, LANES), jnp.int32),
            pltpu.VMEM((2, quarter // LANES, slab + 16 + cap, LANES), f32),
            pltpu.VMEM((PARTS, experts * cap, quarter), bf16),
            dma((ROWS + 1,)), dma((ROWS,)),
        ],
    )(load, saved)
    rows = exchange(mine.reshape(devices, cap, quarter)).reshape(PARTS, experts * cap, quarter)
    logit_grad = call(
        functools.partial(finish_kernel, cap), shape((experts, tokens), f32), [VMEM] * 5, vmem=16,
    )(chosen, scales.astype(f32)[None], router_logits[0].T, codes, rows)
    return logit_grad.T[None]


def solution(mesh):
    placed = (
        P("section", "expert", None),
        P("section", "expert"),
        P("section", "expert", None),
        P("section", "expert", None),
        P("section", "expert", None, None),
    )
    return jax.shard_map(
        local, mesh=mesh, in_specs=placed, out_specs=P("section", "expert", None), check_vma=False
    )
```

```python
import functools

import jax
import jax.numpy as jnp
from jax import lax
from jax.experimental import pallas as pl
from jax.experimental.pallas import tpu as pltpu
from jax.sharding import PartitionSpec as P

ROWS = 8
COLS = 8
PARTS = 4
PART_AT = (0, 2, 1, 3)
WIDE = 1
LANES = 128
VMEM = pl.BlockSpec(memory_space=pltpu.VMEM)
SMEM = pl.BlockSpec(memory_space=pltpu.SMEM)
HBM = pl.BlockSpec(memory_space=pltpu.HBM)


def along_section(x, by):
    n = lax.axis_size("section")
    return lax.ppermute(x, "section", [(i, (i + by) % n) for i in range(n)])


def exchange(x):
    devices = ROWS * COLS
    order = [i * PARTS + q for q in PART_AT for i in range(devices // PARTS)]
    return lax.all_to_all(
        x, "expert", split_axis=0, concat_axis=0, axis_index_groups=[order], tiled=True
    )


def call(kernel, out_shape, in_specs, out_specs=None, flops=0, mib=1, vmem=60, **kw):
    return pl.pallas_call(
        kernel,
        out_shape=out_shape,
        in_specs=in_specs,
        out_specs=jax.tree.map(lambda _: VMEM, out_shape) if out_specs is None else out_specs,
        compiler_params=pltpu.CompilerParams(vmem_limit_bytes=vmem << 20),
        cost_estimate=pl.CostEstimate(flops=flops, bytes_accessed=mib << 20, transcendentals=0),
        **kw,
    )


def count_kernel(routes_ref, out_ref):
    experts = out_ref.shape[0] // PARTS
    ids = lax.broadcasted_iota(jnp.int32, (experts, LANES), 0)
    hit = (routes_ref[0:1] == ids) | (routes_ref[1:2] == ids)
    counts = jnp.sum(hit.astype(jnp.int32), axis=1, keepdims=True)
    for o in range(out_ref.shape[0]):
        out_ref[o] = jnp.broadcast_to(counts[o // PARTS : o // PARTS + 1], (WIDE, LANES))


def slab_kernel(cap, counts_ref, saved_ref, out_ref, held, counts_vmem, wide, slabs, reads, writes):
    devices = ROWS * COLS
    total, tail = saved_ref.shape[0], wide.shape[2]
    reach, depth = tail - cap, total // ROWS
    first = pltpu.make_async_copy(counts_ref, counts_vmem, reads.at[ROWS])
    first.start()
    fetch = [
        pltpu.make_async_copy(
            saved_ref.at[pl.ds(r * depth, depth)], held.at[pl.ds(r * depth, depth)], reads.at[r]
        )
        for r in range(ROWS)
    ]
    for f in fetch:
        f.start()
    first.wait()
    counts = counts_vmem[:, 0].astype(jnp.float32)
    earlier = lax.broadcasted_iota(jnp.int32, (devices, devices), 1) < lax.broadcasted_iota(
        jnp.int32, (devices, devices), 0
    )
    offsets = jnp.dot(
        earlier.astype(jnp.bfloat16), counts.astype(jnp.bfloat16),
        preferred_element_type=jnp.float32,
    ).astype(jnp.int32)
    at = [offsets[d, 0] for d in range(devices)]
    bases = [
        pl.multiple_of(jnp.minimum((at[r * COLS] // 16) * 16, total - reach), 16)
        for r in range(ROWS)
    ]
    for b in range(2):
        wide[b, :, reach:] = jnp.zeros((wide.shape[1], tail - reach, LANES), jnp.float32)
    two = 2 * cap
    store = [
        pltpu.make_async_copy(
            slabs.at[:, pl.ds(r * two, two)], out_ref.at[:, pl.ds(r * two, two)], writes.at[r]
        )
        for r in range(ROWS)
    ]
    for r in range(ROWS):
        b = r % 2
        for f in fetch[:2] if r == 0 else fetch[r + 1 : r + 2]:
            f.wait()
        for k in range(wide.shape[1]):
            wide[b, k, :reach] = held[
                pl.ds(bases[r], reach), k * LANES : (k + 1) * LANES
            ].astype(jnp.float32)
        for k in range(wide.shape[1]):
            for q in range(PARTS):
                rows = [
                    wide[b, k, pl.ds(at[r * COLS + c] - bases[r], cap), :]
                    for c in (q, q + PARTS)
                ]
                slabs[PART_AT[q], r * two : (r + 1) * two, k * LANES : (k + 1) * LANES] = jnp.concatenate(
                    rows, axis=0
                ).astype(jnp.bfloat16)
        store[r].start()
    for w in store:
        w.wait()


def finish_kernel(cap, routes_ref, scales_ref, logits_ref, codes_ref, rows, out_ref):
    experts, tokens = logits_ref.shape
    quarter = rows.shape[2]
    ids = lax.broadcasted_iota(jnp.int32, (experts, tokens), 0)
    hit = (routes_ref[0:1] == ids) | (routes_ref[1:2] == ids)
    upper = lax.broadcasted_iota(jnp.int32, (tokens, tokens), 0) < lax.broadcasted_iota(
        jnp.int32, (tokens, tokens), 1
    )
    before = jnp.dot(
        hit.astype(jnp.float32), upper.astype(jnp.float32), preferred_element_type=jnp.float32
    )
    want = jnp.where(hit, before, -1.0)
    logits = logits_ref[...]
    powers = jnp.exp(logits - jnp.max(logits, axis=0, keepdims=True))
    probs = powers / jnp.sum(powers, axis=0, keepdims=True)
    scores = jnp.zeros((experts * cap, tokens), jnp.float32)
    for q in range(PARTS):
        scores = scores + lax.dot_general(
            rows[PART_AT[q]], codes_ref[:, q * quarter : (q + 1) * quarter], (((1,), (1,)), ((), ())),
            preferred_element_type=jnp.float32,
        )
    line = lax.broadcasted_iota(jnp.int32, (cap, tokens), 0).astype(jnp.float32)
    gate = jnp.concatenate(
        [
            jnp.sum(
                jnp.where(line == want[e : e + 1], scores[e * cap : (e + 1) * cap], 0.0),
                axis=0, keepdims=True,
            )
            for e in range(experts)
        ],
        axis=0,
    )
    gate = gate * scales_ref[...]
    out_ref[...] = probs * (gate - jnp.sum(probs * gate, axis=0, keepdims=True))


def local(grad_codes, grad_scales, routes, router_logits, expert_outputs):
    codes, scales = along_section(grad_codes[0], -1), along_section(grad_scales[0], -1)
    saved = expert_outputs[0, 0]
    devices = ROWS * COLS
    cap = saved.shape[0] // devices
    slab = cap * COLS
    quarter = saved.shape[1]
    tokens = codes.shape[0]
    experts = router_logits.shape[2]
    bf16, f32 = jnp.bfloat16, jnp.float32
    shape, dma = jax.ShapeDtypeStruct, pltpu.SemaphoreType.DMA

    chosen = routes[0].T
    load = lax.all_to_all(
        call(count_kernel, shape((devices, WIDE, LANES), jnp.int32), [VMEM])(chosen),
        "expert", split_axis=0, concat_axis=0, tiled=True,
    )
    mine = call(
        functools.partial(slab_kernel, cap), shape((PARTS, experts * cap, quarter), bf16),
        [HBM, HBM], HBM, mib=6,
        scratch_shapes=[
            pltpu.VMEM(saved.shape, bf16),
            pltpu.VMEM((devices, WIDE, LANES), jnp.int32),
            pltpu.VMEM((2, quarter // LANES, slab + 16 + cap, LANES), f32),
            pltpu.VMEM((PARTS, experts * cap, quarter), bf16),
            dma((ROWS + 1,)), dma((ROWS,)),
        ],
    )(load, saved)
    rows = exchange(mine.reshape(devices, cap, quarter)).reshape(PARTS, experts * cap, quarter)
    logit_grad = call(
        functools.partial(finish_kernel, cap), shape((experts, tokens), f32), [VMEM] * 5, vmem=16,
    )(chosen, scales.astype(f32)[None], router_logits[0].T, codes, rows)
    return logit_grad.T[None]


def solution(mesh):
    placed = (
        P("section", "expert", None),
        P("section", "expert"),
        P("section", "expert", None),
        P("section", "expert", None),
        P("section", "expert", None, None),
    )
    return jax.shard_map(
        local, mesh=mesh, in_specs=placed, out_specs=P("section", "expert", None), check_vma=False
    )
```

```python
import functools

import jax
import jax.numpy as jnp
from jax import lax
from jax.experimental import pallas as pl
from jax.experimental.pallas import tpu as pltpu
from jax.sharding import PartitionSpec as P

ROWS = 8
COLS = 8
PARTS = 4
ROW_AT = (0, 5, 2, 7, 4, 1, 6, 3)
PART_AT = (0, 2, 1, 3)
WIDE = 1
LANES = 128
VMEM = pl.BlockSpec(memory_space=pltpu.VMEM)
SMEM = pl.BlockSpec(memory_space=pltpu.SMEM)
HBM = pl.BlockSpec(memory_space=pltpu.HBM)


def along_section(x, by):
    n = lax.axis_size("section")
    return lax.ppermute(x, "section", [(i, (i + by) % n) for i in range(n)])


def exchange(x):
    devices = ROWS * COLS
    order = [r * COLS + h * PARTS + q for q in PART_AT for r in ROW_AT for h in range(2)]
    return lax.all_to_all(
        x, "expert", split_axis=0, concat_axis=0, axis_index_groups=[order], tiled=True
    )


def call(kernel, out_shape, in_specs, out_specs=None, flops=0, mib=1, vmem=60, **kw):
    return pl.pallas_call(
        kernel,
        out_shape=out_shape,
        in_specs=in_specs,
        out_specs=jax.tree.map(lambda _: VMEM, out_shape) if out_specs is None else out_specs,
        compiler_params=pltpu.CompilerParams(vmem_limit_bytes=vmem << 20),
        cost_estimate=pl.CostEstimate(flops=flops, bytes_accessed=mib << 20, transcendentals=0),
        **kw,
    )


def count_kernel(routes_ref, out_ref):
    experts = out_ref.shape[0] // PARTS
    ids = lax.broadcasted_iota(jnp.int32, (experts, LANES), 0)
    hit = (routes_ref[0:1] == ids) | (routes_ref[1:2] == ids)
    counts = jnp.sum(hit.astype(jnp.int32), axis=1, keepdims=True)
    for o in range(out_ref.shape[0]):
        out_ref[o] = jnp.broadcast_to(counts[o // PARTS : o // PARTS + 1], (WIDE, LANES))


def slab_kernel(cap, counts_ref, saved_ref, out_ref, held, counts_vmem, wide, slabs, reads, writes):
    devices = ROWS * COLS
    total, tail = saved_ref.shape[0], wide.shape[2]
    reach, depth = tail - cap, total // ROWS
    first = pltpu.make_async_copy(counts_ref, counts_vmem, reads.at[ROWS])
    first.start()
    fetch = [
        pltpu.make_async_copy(
            saved_ref.at[pl.ds(r * depth, depth)], held.at[pl.ds(r * depth, depth)], reads.at[r]
        )
        for r in range(ROWS)
    ]
    for f in fetch:
        f.start()
    first.wait()
    counts = counts_vmem[:, 0].astype(jnp.float32)
    earlier = lax.broadcasted_iota(jnp.int32, (devices, devices), 1) < lax.broadcasted_iota(
        jnp.int32, (devices, devices), 0
    )
    offsets = jnp.dot(
        earlier.astype(jnp.bfloat16), counts.astype(jnp.bfloat16),
        preferred_element_type=jnp.float32,
    ).astype(jnp.int32)
    at = [offsets[d, 0] for d in range(devices)]
    bases = [
        pl.multiple_of(jnp.minimum((at[r * COLS] // 16) * 16, total - reach), 16)
        for r in range(ROWS)
    ]
    for b in range(2):
        wide[b, :, reach:] = jnp.zeros((wide.shape[1], tail - reach, LANES), jnp.float32)
    two = 2 * cap
    store = [
        pltpu.make_async_copy(
            slabs.at[:, pl.ds(ROW_AT[r] * two, two)],
            out_ref.at[:, pl.ds(ROW_AT[r] * two, two)], writes.at[r]
        )
        for r in range(ROWS)
    ]
    for r in range(ROWS):
        b = r % 2
        for f in fetch[:2] if r == 0 else fetch[r + 1 : r + 2]:
            f.wait()
        for k in range(wide.shape[1]):
            wide[b, k, :reach] = held[
                pl.ds(bases[r], reach), k * LANES : (k + 1) * LANES
            ].astype(jnp.float32)
        for k in range(wide.shape[1]):
            for q in range(PARTS):
                rows = [
                    wide[b, k, pl.ds(at[r * COLS + c] - bases[r], cap), :]
                    for c in (q, q + PARTS)
                ]
                slabs[PART_AT[q], ROW_AT[r] * two : (ROW_AT[r] + 1) * two, k * LANES : (k + 1) * LANES] = jnp.concatenate(
                    rows, axis=0
                ).astype(jnp.bfloat16)
        store[r].start()
    for w in store:
        w.wait()


def finish_kernel(cap, routes_ref, scales_ref, logits_ref, codes_ref, rows, out_ref):
    experts, tokens = logits_ref.shape
    quarter = rows.shape[2]
    ids = lax.broadcasted_iota(jnp.int32, (experts, tokens), 0)
    hit = (routes_ref[0:1] == ids) | (routes_ref[1:2] == ids)
    upper = lax.broadcasted_iota(jnp.int32, (tokens, tokens), 0) < lax.broadcasted_iota(
        jnp.int32, (tokens, tokens), 1
    )
    before = jnp.dot(
        hit.astype(jnp.float32), upper.astype(jnp.float32), preferred_element_type=jnp.float32
    )
    want = jnp.where(hit, before, -1.0)
    logits = logits_ref[...]
    powers = jnp.exp(logits - jnp.max(logits, axis=0, keepdims=True))
    probs = powers / jnp.sum(powers, axis=0, keepdims=True)
    scores = jnp.zeros((experts * cap, tokens), jnp.float32)
    for q in range(PARTS):
        scores = scores + lax.dot_general(
            rows[PART_AT[q]], codes_ref[:, q * quarter : (q + 1) * quarter], (((1,), (1,)), ((), ())),
            preferred_element_type=jnp.float32,
        )
    line = lax.broadcasted_iota(jnp.int32, (cap, tokens), 0).astype(jnp.float32)
    at = [(2 * ROW_AT[e // 2] + e % 2) * cap for e in range(experts)]
    gate = jnp.concatenate(
        [
            jnp.sum(
                jnp.where(line == want[e : e + 1], scores[at[e] : at[e] + cap], 0.0),
                axis=0, keepdims=True,
            )
            for e in range(experts)
        ],
        axis=0,
    )
    gate = gate * scales_ref[...]
    out_ref[...] = probs * (gate - jnp.sum(probs * gate, axis=0, keepdims=True))


def local(grad_codes, grad_scales, routes, router_logits, expert_outputs):
    codes, scales = along_section(grad_codes[0], -1), along_section(grad_scales[0], -1)
    saved = expert_outputs[0, 0]
    devices = ROWS * COLS
    cap = saved.shape[0] // devices
    slab = cap * COLS
    quarter = saved.shape[1]
    tokens = codes.shape[0]
    experts = router_logits.shape[2]
    bf16, f32 = jnp.bfloat16, jnp.float32
    shape, dma = jax.ShapeDtypeStruct, pltpu.SemaphoreType.DMA

    chosen = routes[0].T
    load = lax.all_to_all(
        call(count_kernel, shape((devices, WIDE, LANES), jnp.int32), [VMEM])(chosen),
        "expert", split_axis=0, concat_axis=0, tiled=True,
    )
    mine = call(
        functools.partial(slab_kernel, cap), shape((PARTS, experts * cap, quarter), bf16),
        [HBM, HBM], HBM, mib=6,
        scratch_shapes=[
            pltpu.VMEM(saved.shape, bf16),
            pltpu.VMEM((devices, WIDE, LANES), jnp.int32),
            pltpu.VMEM((2, quarter // LANES, slab + 16 + cap, LANES), f32),
            pltpu.VMEM((PARTS, experts * cap, quarter), bf16),
            dma((ROWS + 1,)), dma((ROWS,)),
        ],
    )(load, saved)
    rows = exchange(mine.reshape(devices, cap, quarter)).reshape(PARTS, experts * cap, quarter)
    logit_grad = call(
        functools.partial(finish_kernel, cap), shape((experts, tokens), f32), [VMEM] * 5, vmem=16,
    )(chosen, scales.astype(f32)[None], router_logits[0].T, codes, rows)
    return logit_grad.T[None]


def solution(mesh):
    placed = (
        P("section", "expert", None),
        P("section", "expert"),
        P("section", "expert", None),
        P("section", "expert", None),
        P("section", "expert", None, None),
    )
    return jax.shard_map(
        local, mesh=mesh, in_specs=placed, out_specs=P("section", "expert", None), check_vma=False
    )
```
